256 devices in a mesh: grp: 8 (over z), row: 32 (over x, y, core).
Axes of the slice: x: 4, y: 4, z: 8, core: 2. Of those that a mesh axis runs over, the one named last changes fastest.
Arguments:
- pressures: float32 [64, 4194304], P('row', 'grp'), may hold values from -400 to 400
Outputs:
- factor: float32 [64, 64], replicated
- modes: float32 [64, 4194304], P(None, ('grp', 'row'))
The draws below stay inside these ranges and needn't reach their ends.
All inputs are finite; a program needn't handle non-finite values.
Results may differ from the reference program's by a relative error of at most 0.0003.
Values sent between devices are 32-bit elements; how exact they have to be, the bound alone decides.
A program may use at most 64 MiB of HBM per device.

```python
import jax
import jax.numpy as jnp
from jax import lax

SNAP = 64
ROWS = 16384
NSTEPS = 16
FACES = 4194304


def draw_pressures(key, part):
    key = jax.random.fold_in(key, 7)
    first, second, third = jax.random.split(key, 3)
    face_scale = jnp.exp(jax.random.uniform(first, (1, FACES), jnp.float32, 0.0, 2.302585))
    snap_scale = jnp.exp(jax.random.uniform(second, (SNAP, 1), jnp.float32, 0.0, 2.302585))
    base = jnp.clip(jax.random.normal(third, (SNAP, FACES), jnp.float32), -3.9, 3.9)
    return (base * face_scale * snap_scale).astype(jnp.float32)


def setup_inputs(seed: int = 0) -> dict:
    key_list = jax.random.split(jax.random.key(seed), 2)
    pressures = draw_pressures(jax.random.fold_in(key_list[1], 71), 0)
    return {"pressures": pressures}


def reference(pressures):
    blocks = FACES // ROWS

    def absorb(upper, index):
        start = (index * ROWS).astype(jnp.int32)
        block = lax.dynamic_slice_in_dim(pressures, start, ROWS, 1)
        stacked = jnp.concatenate([upper, block.T], axis=0)
        return (jnp.linalg.qr(stacked, mode='r'), None)
    upper, unused = lax.scan(absorb, jnp.zeros((SNAP, SNAP), jnp.float32), jnp.arange(blocks, dtype=jnp.int32))
    signs = jnp.where(jnp.diagonal(upper) < 0, -1.0, 1.0).astype(jnp.float32)
    upper = upper * signs[:, None]
    root = jnp.sqrt(jnp.float32(FACES))
    factor = upper / root
    rotation = upper / jnp.sqrt(jnp.sum(upper * upper) + 1e-06)
    for step in range(NSTEPS):
        square = jnp.dot(rotation.T, rotation, precision=lax.Precision.HIGHEST)
        rotation = 1.5 * rotation - 0.5 * jnp.dot(rotation, square, precision=lax.Precision.HIGHEST)
    mixer = jax.scipy.linalg.solve_triangular(upper, rotation, lower=False) * root
    modes = jnp.dot(mixer.T, pressures, precision=lax.Precision.HIGHEST)
    return (factor, modes)
```

```python
import jax
import jax.numpy as jnp
from jax import lax
from jax.experimental import pallas as pl
from jax.experimental.pallas import tpu as pltpu
from jax.sharding import PartitionSpec as P

NSTEPS = 16
SNAP = 64
ROWS = 16384
FACES = 4194304
CHUNKS = 8
WIDTH = ROWS // CHUNKS
TILE = 1024
MESH = pl.DeviceIdType.MESH
f32, bf16 = jnp.float32, jnp.bfloat16


def split3(a):
    high = a.astype(bf16)
    rest = a - high.astype(f32)
    mid = rest.astype(bf16)
    low = (rest - mid.astype(f32)).astype(bf16)
    return high, mid, low


def sum16(buf):
    eight = (buf[0:8, :] + buf[8:16, :]) + (buf[16:24, :] + buf[24:32, :])
    return (eight[0:2, :] + eight[2:4, :]) + (eight[4:6, :] + eight[6:8, :])


def gather_kernel(x_ref, land, g_ref, packed, buf1, part1, buf2, part2, buf3,
                  send_sem, recv_sem, own_sem, red_send, red_recv):
    grp, me = lax.axis_index("grp"), lax.axis_index("row")
    mx, my, mc = me // 8, (me // 2) % 4, me % 2

    barrier = pltpu.get_barrier_semaphore()

    def greet_row(k, _):
        pl.semaphore_signal(barrier, inc=1, device_id=(grp, (me + k) % 32), device_id_type=MESH)
        return 0

    def greet_grp(k, _):
        g, c = (grp + k // 2) % 8, (mc + k % 2) % 2
        pl.semaphore_signal(barrier, inc=1, device_id=(g, me - mc + c), device_id_type=MESH)
        return 0

    lax.fori_loop(1, 32, greet_row, 0)
    lax.fori_loop(2, 16, greet_grp, 0)
    pl.semaphore_wait(barrier, 31 + 14)

    def rows_of(i, c):
        return land.at[pl.ds(pl.multiple_of(2 * i, 2), 2), pl.ds(c * WIDTH, WIDTH)]

    def faces_of(j, c):
        return x_ref.at[:, pl.ds(pl.multiple_of(j * ROWS + c * WIDTH, WIDTH), WIDTH)]

    def wait_bytes(columns, sem):
        size = x_ref.at[:, pl.ds(0, columns)]
        pltpu.make_async_copy(size, size, sem).wait()

    def own(c):
        return pltpu.make_async_copy(faces_of(me, c), rows_of(me, c), own_sem.at[c])

    for c in range(CHUNKS):
        def send(q, _):
            k = (q * (13 + 6 * mc)) % 32
            j = ((mx + k // 8) % 4) * 8 + ((my + (k // 2) % 4) % 4) * 2 + (mc + k % 2) % 2
            pltpu.make_async_remote_copy(
                src_ref=faces_of(j, c), dst_ref=rows_of(me, c), send_sem=send_sem, recv_sem=recv_sem.at[c],
                device_id=(grp, j), device_id_type=MESH).start()
            return 0
        lax.fori_loop(1, 32, send, 0)
        own(c).start()

    total = jnp.zeros((3 * SNAP, 3 * SNAP), f32)
    for c in range(CHUNKS):
        own(c).wait()
        wait_bytes(31 * WIDTH, recv_sem.at[c])
        parts = jnp.concatenate(split3(land[:, c * WIDTH:(c + 1) * WIDTH]), axis=0)
        total = total + lax.dot_general(parts, parts, (((1,), (1,)), ((), ())), preferred_element_type=f32)
    a, b = SNAP, 2 * SNAP
    gram = total[:a, :a] + ((total[a:b, :a] + total[:a, a:b]) + (total[b:, :a] + total[:a, b:] + total[a:b, a:b]))

    packed[...] = jnp.concatenate([gram[:32, :], gram[32:, :]], axis=1)
    line = grp * 2 + mc

    def to_line(source, place, n, step):
        def send(k, _):
            t = (line + k) % 16
            pltpu.make_async_remote_copy(
                src_ref=source(t), dst_ref=place.at[pl.ds(pl.multiple_of(2 * line, 2), 2), :],
                send_sem=red_send.at[step], recv_sem=red_recv.at[step],
                device_id=(t // 2, me - mc + t % 2), device_id_type=MESH).start()
            return 0
        lax.fori_loop(1, 16, send, 0)

    def finish(step):
        wait_bytes(15 * 128, red_recv.at[step])

    def keep(source, place, index, step):
        copy = pltpu.make_async_copy(source, place.at[pl.ds(pl.multiple_of(2 * index, 2), 2), :], own_sem.at[step])
        copy.start()
        return copy

    kept = keep(packed.at[pl.ds(pl.multiple_of(2 * line, 2), 2), :], buf1, line, 0)
    to_line(lambda t: packed.at[pl.ds(pl.multiple_of(2 * t, 2), 2), :], buf1, 16, 0)
    kept.wait()
    finish(0)
    part1[...] = sum16(buf1)

    chip = me // 2
    kept = keep(part1, buf2, chip, 1)

    def to_plane(k, _):
        t = (chip + k) % 16
        pltpu.make_async_remote_copy(
            src_ref=part1, dst_ref=buf2.at[pl.ds(pl.multiple_of(2 * chip, 2), 2), :],
            send_sem=red_send.at[1], recv_sem=red_recv.at[1],
            device_id=(grp, 2 * t + mc), device_id_type=MESH).start()
        return 0
    lax.fori_loop(1, 16, to_plane, 0)
    kept.wait()
    finish(1)
    part2[...] = sum16(buf2)

    kept = keep(part2, buf3, line, 2)
    to_line(lambda t: part2, buf3, 16, 2)
    kept.wait()
    finish(2)
    g_ref[...] = jnp.concatenate([buf3[:, :SNAP], buf3[:, SNAP:]], axis=0)

    for step in range(3):
        wait_bytes(15 * 128, red_send.at[step])
    wait_bytes(31 * ROWS, send_sem)


def modes_kernel(x_ref, g_ref, factor_ref, modes_hbm, out, sem):
    def times(p, q):
        return jnp.dot(p, q, precision=lax.Precision.HIGHEST, preferred_element_type=f32)

    gram = g_ref[...]
    down = lax.broadcasted_iota(jnp.int32, (SNAP, SNAP), 0)
    across = lax.broadcasted_iota(jnp.int32, (SNAP, SNAP), 1)
    eye = jnp.where(down == across, 1.0, 0.0).astype(f32)
    lane = lax.broadcasted_iota(jnp.int32, (1, SNAP), 1)
    square = jnp.sum(jnp.sum(gram * eye, axis=0, keepdims=True), axis=1, keepdims=True) + 1e-6
    shape, inverse = gram / square, eye
    rest, rows = gram, []
    for step in range(NSTEPS):
        factor = 1.5 * eye - 0.5 * shape
        if step < NSTEPS - 1:
            shape_square = times(shape, shape)
        inverse = factor if step == 0 else times(inverse, factor)
        if step < NSTEPS - 1:
            shape = times(1.5 * shape - 0.5 * shape_square, factor)
        for k in range(step * SNAP // NSTEPS, (step + 1) * SNAP // NSTEPS):
            scale = lax.rsqrt(rest[k:k + 1, k:k + 1])
            row = rest[k:k + 1, :] * scale
            rows.append(jnp.where(lane >= k, row, 0.0))
            rest = rest - (rest[:, k:k + 1] * scale) * row
    root = float(FACES) ** 0.5
    factor_ref[...] = jnp.concatenate(rows, axis=0) * (1.0 / root)
    mixer = inverse * (root * lax.rsqrt(square))
    high, mid, low = split3(mixer)
    left = jnp.concatenate([high, mid, low, high, mid, high], axis=1)

    def tile(i, _):
        cols = pl.ds(pl.multiple_of(i * TILE, TILE), TILE)
        h, m, l = split3(x_ref[:, cols])
        out[:, cols] = jnp.dot(left, jnp.concatenate([h, h, h, m, m, l], axis=0), preferred_element_type=f32)
        pltpu.make_async_copy(out.at[:, cols], modes_hbm.at[:, cols], sem).start()
        return 0
    lax.fori_loop(0, ROWS // TILE, tile, 0, unroll=2)
    pltpu.make_async_copy(out, modes_hbm, sem).wait()


def shards(pressures):
    vmem = pl.BlockSpec(memory_space=pltpu.VMEM)
    anywhere = pl.BlockSpec(memory_space=pl.ANY)
    local_rows, gram = pl.pallas_call(
        gather_kernel,
        out_shape=(jax.ShapeDtypeStruct((SNAP, ROWS), f32), jax.ShapeDtypeStruct((SNAP, SNAP), f32)),
        in_specs=[anywhere],
        out_specs=(vmem, vmem),
        scratch_shapes=[
            pltpu.VMEM((32, 128), f32), pltpu.VMEM((32, 128), f32), pltpu.VMEM((2, 128), f32),
            pltpu.VMEM((32, 128), f32), pltpu.VMEM((2, 128), f32), pltpu.VMEM((32, 128), f32),
            pltpu.SemaphoreType.DMA, pltpu.SemaphoreType.DMA((CHUNKS,)), pltpu.SemaphoreType.DMA((CHUNKS,)),
            pltpu.SemaphoreType.DMA((3,)), pltpu.SemaphoreType.DMA((3,)),
        ],
        compiler_params=pltpu.CompilerParams(collective_id=0, has_side_effects=True, vmem_limit_bytes=40 << 20),
        cost_estimate=pl.CostEstimate(flops=2 * 192 * 192 * ROWS, bytes_accessed=8 << 20, transcendentals=0),
    )(pressures)
    return pl.pallas_call(
        modes_kernel,
        out_shape=(jax.ShapeDtypeStruct((SNAP, SNAP), f32), jax.ShapeDtypeStruct((SNAP, ROWS), f32)),
        in_specs=[vmem, vmem],
        out_specs=(vmem, anywhere),
        scratch_shapes=[pltpu.VMEM((SNAP, ROWS), f32), pltpu.SemaphoreType.DMA],
        compiler_params=pltpu.CompilerParams(vmem_limit_bytes=40 << 20),
        cost_estimate=pl.CostEstimate(flops=2 * 384 * 64 * ROWS, bytes_accessed=8 << 20, transcendentals=0),
    )(local_rows, gram)


def solution(mesh):
    in_specs = (P("row", "grp"),)
    out_specs = (P(), P(None, ("grp", "row")))
    return jax.shard_map(shards, mesh=mesh, in_specs=in_specs, out_specs=out_specs, check_vma=False)
```

```python
import jax
import jax.numpy as jnp
from jax import lax
from jax.experimental import pallas as pl
from jax.experimental.pallas import tpu as pltpu
from jax.sharding import PartitionSpec as P

NSTEPS = 16
SNAP = 64
ROWS = 16384
FACES = 4194304
CHUNKS = 8
WIDTH = ROWS // CHUNKS
TILE = 1024
MESH = pl.DeviceIdType.MESH
f32, bf16 = jnp.float32, jnp.bfloat16


def split3(a):
    high = a.astype(bf16)
    rest = a - high.astype(f32)
    mid = rest.astype(bf16)
    low = (rest - mid.astype(f32)).astype(bf16)
    return high, mid, low


NEAR = [(0, 0, 1), (1, 0, 0), (0, 1, 0), (3, 0, 0), (0, 3, 0)]
NEXT = [(1, 1, 0), (3, 3, 0), (1, 3, 0), (3, 1, 0), (2, 0, 0), (0, 2, 0), (1, 0, 1), (0, 1, 1), (3, 0, 1), (0, 3, 1)]
FAR = [(2, 2, 1), (2, 2, 0), (2, 1, 0), (1, 2, 0), (2, 3, 0), (3, 2, 0), (2, 1, 1), (1, 2, 1), (2, 3, 1), (3, 2, 1),
       (1, 1, 1), (3, 3, 1), (1, 3, 1), (3, 1, 1), (2, 0, 1), (0, 2, 1)]


def added(buf, count):
    terms = [buf[i] for i in range(count)]
    while len(terms) > 1:
        terms = [p + q for p, q in zip(terms[::2], terms[1::2])]
    return terms[0]


def gather_kernel(x_ref, land, g_ref, packed, pair, half, plane_buf, line_buf, plane_sum, line_sum,
                  send_sem, recv_sem, own_sem, row_sem, grp_sem, red_send, red_recv):
    grp, me = lax.axis_index("grp"), lax.axis_index("row")
    mx, my, mc = me // 8, (me // 2) % 4, me % 2
    chip = me // 2
    at_x = [((mx + d) % 4) * 8 for d in range(4)]
    at_y = [((my + d) % 4) * 2 for d in range(4)]
    at_core = [mc, 1 - mc]
    above, below = (grp + 1) % 8, (grp + 7) % 8

    def row_place(offset):
        dx, dy, dc = offset
        return at_x[dx] + at_y[dy] + at_core[dc]

    def signal_near(sem):
        for offset in NEAR:
            pl.semaphore_signal(sem, inc=1, device_id=(grp, row_place(offset)), device_id_type=MESH)

    def signal_line(sem):
        pl.semaphore_signal(sem, inc=1, device_id=(above, me), device_id_type=MESH)
        pl.semaphore_signal(sem, inc=1, device_id=(below, me), device_id_type=MESH)

    barrier = pltpu.get_barrier_semaphore()
    signal_near(barrier)
    signal_line(barrier)
    pl.semaphore_wait(barrier, len(NEAR) + 2)
    signal_near(row_sem.at[0])
    signal_line(grp_sem.at[0])

    def rows_of(i, c):
        return land.at[pl.ds(pl.multiple_of(2 * i, 2), 2), pl.ds(pl.multiple_of(c * WIDTH, WIDTH), WIDTH)]

    def faces_of(j, c):
        return x_ref.at[:, pl.ds(pl.multiple_of(j * ROWS + c * WIDTH, WIDTH), WIDTH)]

    def wait_bytes(columns, sem):
        size = x_ref.at[:, pl.ds(0, columns)]
        pltpu.make_async_copy(size, size, sem).wait()

    def own(c):
        return pltpu.make_async_copy(faces_of(me, c), rows_of(me, c), own_sem.at[c])

    def send_chunks(first, last, offsets):
        def send(c, _):
            for offset in offsets:
                j = row_place(offset)
                pltpu.make_async_remote_copy(
                    src_ref=faces_of(j, c), dst_ref=rows_of(me, c), send_sem=send_sem, recv_sem=recv_sem.at[c],
                    device_id=(grp, j), device_id_type=MESH).start()
            return 0
        lax.fori_loop(first, last, send, 0)

    def next_round(r):
        pl.semaphore_wait(row_sem.at[r], len(NEAR))
        if r < 3:
            signal_near(row_sem.at[r + 1])

    send_chunks(0, CHUNKS, NEAR)
    next_round(0)
    send_chunks(0, 2, NEXT)
    next_round(1)
    send_chunks(2, 4, NEXT)
    next_round(2)
    send_chunks(4, CHUNKS, NEXT)
    next_round(3)
    send_chunks(0, CHUNKS, FAR)
    for c in range(CHUNKS):
        own(c).start()
    for r in range(3):
        pl.semaphore_wait(grp_sem.at[r], 2)
        if r < 2:
            signal_line(grp_sem.at[r + 1])

    total = jnp.zeros((3 * SNAP, 3 * SNAP), f32)
    for c in range(CHUNKS):
        own(c).wait()
        wait_bytes(31 * WIDTH, recv_sem.at[c])
        parts = jnp.concatenate(split3(land[:, c * WIDTH:(c + 1) * WIDTH]), axis=0)
        total = total + lax.dot_general(parts, parts, (((1,), (1,)), ((), ())), preferred_element_type=f32)
    a, b = SNAP, 2 * SNAP
    gram = total[:a, :a] + ((total[a:b, :a] + total[:a, a:b]) + (total[b:, :a] + total[:a, b:] + total[a:b, a:b]))

    def post(source, target, step, device):
        pltpu.make_async_remote_copy(
            src_ref=source, dst_ref=target, send_sem=red_send.at[step], recv_sem=red_recv.at[step],
            device_id=device, device_id_type=MESH).start()

    def to_plane(source, q, step):
        for dx in range(4):
            for dy in range(4):
                if dx or dy:
                    post(source, plane_buf.at[q, chip], step, (grp, at_x[dx] + at_y[dy] + mc))

    def to_line(source, q, step):
        for d in range(1, 8):
            post(source, line_buf.at[q, grp], step, ((grp + d) % 8, me))

    packed[...] = jnp.concatenate([gram[:32, :], gram[32:, :]], axis=1).reshape(2, 16, 128)
    post(packed.at[1 - mc], pair.at[0], 0, (grp, at_x[0] + at_y[0] + at_core[1]))
    wait_bytes(1024, red_recv.at[0])
    mine = packed[mc] + pair[0]
    plane_sum[0] = mine[:8]
    line_sum[1] = mine[8:]
    to_line(line_sum.at[1], 1, 2)
    to_plane(plane_sum.at[0], 0, 1)
    plane_buf[0, chip] = mine[:8]
    line_buf[1, grp] = mine[8:]
    wait_bytes(7 * 512, red_recv.at[2])
    quarter = added(line_buf.at[1], 8)
    plane_sum[1] = quarter
    to_plane(plane_sum.at[1], 1, 4)
    plane_buf[1, chip] = quarter
    wait_bytes(15 * 512, red_recv.at[1])
    quarter = added(plane_buf.at[0], 16)
    line_sum[0] = quarter
    to_line(line_sum.at[0], 0, 3)
    line_buf[0, grp] = quarter
    wait_bytes(15 * 512, red_recv.at[4])
    half[mc, 8:16] = added(plane_buf.at[1], 16)
    wait_bytes(7 * 512, red_recv.at[3])
    half[mc, 0:8] = added(line_buf.at[0], 8)
    post(half.at[mc], half.at[mc], 5, (grp, at_x[0] + at_y[0] + at_core[1]))
    wait_bytes(1024, red_recv.at[5])
    summed = half[...].reshape(32, 128)
    g_ref[...] = jnp.concatenate([summed[:, :SNAP], summed[:, SNAP:]], axis=0)

    for step, columns in enumerate((1024, 15 * 512, 7 * 512, 7 * 512, 15 * 512, 1024)):
        wait_bytes(columns, red_send.at[step])
    wait_bytes(31 * ROWS, send_sem)


def modes_kernel(x_ref, g_ref, factor_ref, modes_hbm, out, sem):
    def times(p, q):
        return jnp.dot(p, q, precision=lax.Precision.HIGHEST, preferred_element_type=f32)

    gram = g_ref[...]
    down = lax.broadcasted_iota(jnp.int32, (SNAP, SNAP), 0)
    across = lax.broadcasted_iota(jnp.int32, (SNAP, SNAP), 1)
    eye = jnp.where(down == across, 1.0, 0.0).astype(f32)
    lane = lax.broadcasted_iota(jnp.int32, (1, SNAP), 1)
    square = jnp.sum(jnp.sum(gram * eye, axis=0, keepdims=True), axis=1, keepdims=True) + 1e-6
    shape, inverse = gram / square, eye
    rest, rows = gram, []
    for step in range(NSTEPS):
        factor = 1.5 * eye - 0.5 * shape
        if step < NSTEPS - 1:
            shape_square = times(shape, shape)
        inverse = factor if step == 0 else times(inverse, factor)
        if step < NSTEPS - 1:
            shape = times(1.5 * shape - 0.5 * shape_square, factor)
        for k in range(step * SNAP // NSTEPS, (step + 1) * SNAP // NSTEPS):
            scale = lax.rsqrt(rest[k:k + 1, k:k + 1])
            row = rest[k:k + 1, :] * scale
            rows.append(jnp.where(lane >= k, row, 0.0))
            rest = rest - (rest[:, k:k + 1] * scale) * row
    root = float(FACES) ** 0.5
    factor_ref[...] = jnp.concatenate(rows, axis=0) * (1.0 / root)
    mixer = inverse * (root * lax.rsqrt(square))
    high, mid, low = split3(mixer)
    none = jnp.zeros_like(high)
    left = jnp.concatenate([jnp.concatenate([high, high, high, mid], axis=1),
                            jnp.concatenate([low, mid, none, none], axis=1)], axis=0)

    def tile(i, _):
        cols = pl.ds(pl.multiple_of(i * TILE, TILE), TILE)
        h, m, l = split3(x_ref[:, cols])
        both = jnp.dot(left, jnp.concatenate([h, m, l, h], axis=0), preferred_element_type=f32)
        out[:, cols] = both[:SNAP] + both[SNAP:]
        pltpu.make_async_copy(out.at[:, cols], modes_hbm.at[:, cols], sem).start()
        return 0
    lax.fori_loop(0, ROWS // TILE, tile, 0, unroll=ROWS // TILE)
    pltpu.make_async_copy(out, modes_hbm, sem).wait()


def shards(pressures):
    vmem = pl.BlockSpec(memory_space=pltpu.VMEM)
    anywhere = pl.BlockSpec(memory_space=pl.ANY)
    local_rows, gram = pl.pallas_call(
        gather_kernel,
        out_shape=(jax.ShapeDtypeStruct((SNAP, ROWS), f32), jax.ShapeDtypeStruct((SNAP, SNAP), f32)),
        in_specs=[anywhere],
        out_specs=(vmem, vmem),
        scratch_shapes=[
            pltpu.VMEM((2, 16, 128), f32), pltpu.VMEM((1, 16, 128), f32), pltpu.VMEM((2, 16, 128), f32),
            pltpu.VMEM((2, 16, 8, 128), f32), pltpu.VMEM((2, 8, 8, 128), f32),
            pltpu.VMEM((2, 8, 128), f32), pltpu.VMEM((2, 8, 128), f32),
            pltpu.SemaphoreType.DMA, pltpu.SemaphoreType.DMA((CHUNKS,)), pltpu.SemaphoreType.DMA((CHUNKS,)),
            pltpu.SemaphoreType.REGULAR((4,)), pltpu.SemaphoreType.REGULAR((3,)),
            pltpu.SemaphoreType.DMA((6,)), pltpu.SemaphoreType.DMA((6,)),
        ],
        compiler_params=pltpu.CompilerParams(collective_id=0, has_side_effects=True, vmem_limit_bytes=40 << 20),
        cost_estimate=pl.CostEstimate(flops=2 * 192 * 192 * ROWS, bytes_accessed=8 << 20, transcendentals=0),
    )(pressures)
    return pl.pallas_call(
        modes_kernel,
        out_shape=(jax.ShapeDtypeStruct((SNAP, SNAP), f32), jax.ShapeDtypeStruct((SNAP, ROWS), f32)),
        in_specs=[vmem, vmem],
        out_specs=(vmem, anywhere),
        scratch_shapes=[pltpu.VMEM((SNAP, ROWS), f32), pltpu.SemaphoreType.DMA],
        compiler_params=pltpu.CompilerParams(vmem_limit_bytes=40 << 20),
        cost_estimate=pl.CostEstimate(flops=2 * 384 * 64 * ROWS, bytes_accessed=8 << 20, transcendentals=0),
    )(local_rows, gram)


def solution(mesh):
    in_specs = (P("row", "grp"),)
    out_specs = (P(), P(None, ("grp", "row")))
    return jax.shard_map(shards, mesh=mesh, in_specs=in_specs, out_specs=out_specs, check_vma=False)
```

```python
import jax
import jax.numpy as jnp
from jax import lax
from jax.experimental import pallas as pl
from jax.experimental.pallas import tpu as pltpu
from jax.sharding import PartitionSpec as P

NSTEPS = 16
SNAP = 64
ROWS = 16384
FACES = 4194304
CHUNKS = 8
WIDTH = ROWS // CHUNKS
TILE = 1024
MESH = pl.DeviceIdType.MESH
f32, bf16 = jnp.float32, jnp.bfloat16


def split3(a):
    high = a.astype(bf16)
    rest = a - high.astype(f32)
    mid = rest.astype(bf16)
    low = (rest - mid.astype(f32)).astype(bf16)
    return high, mid, low


NEAR = [(0, 0, 1), (1, 0, 0), (0, 1, 0), (3, 0, 0), (0, 3, 0)]
NEXT = [(1, 1, 0), (3, 3, 0), (1, 3, 0), (3, 1, 0), (2, 0, 0), (0, 2, 0), (1, 0, 1), (0, 1, 1), (3, 0, 1), (0, 3, 1)]
FAR = [(2, 2, 1), (2, 2, 0), (2, 1, 0), (1, 2, 0), (2, 3, 0), (3, 2, 0), (2, 1, 1), (1, 2, 1), (2, 3, 1), (3, 2, 1),
       (1, 1, 1), (3, 3, 1), (1, 3, 1), (3, 1, 1), (2, 0, 1), (0, 2, 1)]


FAR_CHIPS = [(2, 2), (2, 1), (1, 2), (2, 3), (3, 2), (1, 1), (3, 3), (1, 3), (3, 1), (2, 0), (0, 2), (1, 0), (0, 1), (3, 0), (0, 3)]


def added(buf, count):
    terms = [buf[i] for i in range(count)]
    while len(terms) > 1:
        terms = [p + q for p, q in zip(terms[::2], terms[1::2])]
    return terms[0]


def gather_kernel(x_ref, land, g_ref, packed, pair, half, plane_buf, line_buf, plane_sum, line_sum,
                  send_sem, recv_sem, own_sem, row_sem, grp_sem, red_send, red_recv):
    grp, me = lax.axis_index("grp"), lax.axis_index("row")
    mx, my, mc = me // 8, (me // 2) % 4, me % 2
    chip = me // 2
    at_x = [((mx + d) % 4) * 8 for d in range(4)]
    at_y = [((my + d) % 4) * 2 for d in range(4)]
    at_core = [mc, 1 - mc]
    above, below = (grp + 1) % 8, (grp + 7) % 8

    def row_place(offset):
        dx, dy, dc = offset
        return at_x[dx] + at_y[dy] + at_core[dc]

    def signal_near(sem):
        for offset in NEAR:
            pl.semaphore_signal(sem, inc=1, device_id=(grp, row_place(offset)), device_id_type=MESH)

    def signal_line(sem):
        pl.semaphore_signal(sem, inc=1, device_id=(above, me), device_id_type=MESH)
        pl.semaphore_signal(sem, inc=1, device_id=(below, me), device_id_type=MESH)

    barrier = pltpu.get_barrier_semaphore()
    signal_near(barrier)
    signal_line(barrier)
    pl.semaphore_wait(barrier, len(NEAR) + 2)
    signal_near(row_sem.at[0])
    signal_line(grp_sem.at[0])

    def rows_of(i, c):
        return land.at[pl.ds(pl.multiple_of(2 * i, 2), 2), pl.ds(pl.multiple_of(c * WIDTH, WIDTH), WIDTH)]

    def faces_of(j, c):
        return x_ref.at[:, pl.ds(pl.multiple_of(j * ROWS + c * WIDTH, WIDTH), WIDTH)]

    def wait_bytes(columns, sem):
        size = x_ref.at[:, pl.ds(0, columns)]
        pltpu.make_async_copy(size, size, sem).wait()

    def own(c):
        return pltpu.make_async_copy(faces_of(me, c), rows_of(me, c), own_sem.at[c])

    def send_chunks(first, last, offsets):
        def send(c, _):
            for offset in offsets:
                j = row_place(offset)
                pltpu.make_async_remote_copy(
                    src_ref=faces_of(j, c), dst_ref=rows_of(me, c), send_sem=send_sem, recv_sem=recv_sem.at[c],
                    device_id=(grp, j), device_id_type=MESH).start()
            return 0
        lax.fori_loop(first, last, send, 0)

    def next_round(r):
        pl.semaphore_wait(row_sem.at[r], len(NEAR))
        if r < 3:
            signal_near(row_sem.at[r + 1])

    send_chunks(0, CHUNKS, NEAR)
    next_round(0)
    send_chunks(0, 2, NEXT)
    next_round(1)
    send_chunks(2, 4, NEXT)
    next_round(2)
    send_chunks(4, CHUNKS, NEXT)
    next_round(3)
    send_chunks(0, CHUNKS, FAR)
    for c in range(CHUNKS):
        own(c).start()
    for r in range(3):
        pl.semaphore_wait(grp_sem.at[r], 2)
        if r < 2:
            signal_line(grp_sem.at[r + 1])

    total = jnp.zeros((3 * SNAP, 3 * SNAP), f32)
    for c in range(CHUNKS):
        own(c).wait()
        wait_bytes(31 * WIDTH, recv_sem.at[c])
        parts = jnp.concatenate(split3(land[:, c * WIDTH:(c + 1) * WIDTH]), axis=0)
        total = total + lax.dot_general(parts, parts, (((1,), (1,)), ((), ())), preferred_element_type=f32)
    a, b = SNAP, 2 * SNAP
    gram = total[:a, :a] + ((total[a:b, :a] + total[:a, a:b]) + (total[b:, :a] + total[:a, b:] + total[a:b, a:b]))

    def post(source, target, step, device):
        pltpu.make_async_remote_copy(
            src_ref=source, dst_ref=target, send_sem=red_send.at[step], recv_sem=red_recv.at[step],
            device_id=device, device_id_type=MESH).start()

    def to_plane(source, q, step):
        for dx, dy in FAR_CHIPS:
            post(source, plane_buf.at[q, chip], step, (grp, at_x[dx] + at_y[dy] + mc))

    def to_line(source, q, step):
        for d in (4, 3, 5, 2, 6, 1, 7):
            post(source, line_buf.at[q, grp], step, ((grp + d) % 8, me))

    packed[...] = jnp.concatenate([gram[:32, :], gram[32:, :]], axis=1).reshape(2, 16, 128)
    post(packed.at[1 - mc], pair.at[0], 0, (grp, at_x[0] + at_y[0] + at_core[1]))
    wait_bytes(1024, red_recv.at[0])
    mine = packed[mc] + pair[0]
    plane_sum[0] = mine[:8]
    line_sum[1] = mine[8:]
    to_line(line_sum.at[1], 1, 2)
    to_plane(plane_sum.at[0], 0, 1)
    plane_buf[0, chip] = mine[:8]
    line_buf[1, grp] = mine[8:]
    wait_bytes(7 * 512, red_recv.at[2])
    quarter = added(line_buf.at[1], 8)
    plane_sum[1] = quarter
    to_plane(plane_sum.at[1], 1, 4)
    plane_buf[1, chip] = quarter
    wait_bytes(15 * 512, red_recv.at[1])
    quarter = added(plane_buf.at[0], 16)
    line_sum[0] = quarter
    to_line(line_sum.at[0], 0, 3)
    line_buf[0, grp] = quarter
    wait_bytes(15 * 512, red_recv.at[4])
    half[mc, 8:16] = added(plane_buf.at[1], 16)
    wait_bytes(7 * 512, red_recv.at[3])
    half[mc, 0:8] = added(line_buf.at[0], 8)
    post(half.at[mc], half.at[mc], 5, (grp, at_x[0] + at_y[0] + at_core[1]))
    wait_bytes(1024, red_recv.at[5])
    summed = half[...].reshape(32, 128)
    g_ref[...] = jnp.concatenate([summed[:, :SNAP], summed[:, SNAP:]], axis=0)

    for step, columns in enumerate((1024, 15 * 512, 7 * 512, 7 * 512, 15 * 512, 1024)):
        wait_bytes(columns, red_send.at[step])
    wait_bytes(31 * ROWS, send_sem)


def modes_kernel(x_ref, g_ref, factor_ref, modes_hbm, out, sem):
    def times(p, q):
        return jnp.dot(p, q, precision=lax.Precision.HIGHEST, preferred_element_type=f32)

    gram = g_ref[...]
    down = lax.broadcasted_iota(jnp.int32, (SNAP, SNAP), 0)
    across = lax.broadcasted_iota(jnp.int32, (SNAP, SNAP), 1)
    eye = jnp.where(down == across, 1.0, 0.0).astype(f32)
    lane = lax.broadcasted_iota(jnp.int32, (1, SNAP), 1)
    square = jnp.sum(jnp.sum(gram * eye, axis=0, keepdims=True), axis=1, keepdims=True) + 1e-6
    shape, inverse = gram / square, eye
    rest, rows = gram, []
    for step in range(NSTEPS):
        factor = 1.5 * eye - 0.5 * shape
        if step < NSTEPS - 1:
            shape_square = times(shape, shape)
        inverse = factor if step == 0 else times(inverse, factor)
        if step < NSTEPS - 1:
            shape = times(1.5 * shape - 0.5 * shape_square, factor)
        for k in range(step * SNAP // NSTEPS, (step + 1) * SNAP // NSTEPS):
            scale = lax.rsqrt(rest[k:k + 1, k:k + 1])
            row = rest[k:k + 1, :] * scale
            rows.append(jnp.where(lane >= k, row, 0.0))
            rest = rest - (rest[:, k:k + 1] * scale) * row
    root = float(FACES) ** 0.5
    factor_ref[...] = jnp.concatenate(rows, axis=0) * (1.0 / root)
    mixer = inverse * (root * lax.rsqrt(square))
    high, mid, low = split3(mixer)
    none = jnp.zeros_like(high)
    left = jnp.concatenate([jnp.concatenate([high, high, high, mid], axis=1),
                            jnp.concatenate([low, mid, none, none], axis=1)], axis=0)

    def tile(i, _):
        cols = pl.ds(pl.multiple_of(i * TILE, TILE), TILE)
        h, m, l = split3(x_ref[:, cols])
        both = jnp.dot(left, jnp.concatenate([h, m, l, h], axis=0), preferred_element_type=f32)
        out[:, cols] = both[:SNAP] + both[SNAP:]
        pltpu.make_async_copy(out.at[:, cols], modes_hbm.at[:, cols], sem).start()
        return 0
    lax.fori_loop(0, ROWS // TILE, tile, 0, unroll=ROWS // TILE)
    pltpu.make_async_copy(out, modes_hbm, sem).wait()


def shards(pressures):
    vmem = pl.BlockSpec(memory_space=pltpu.VMEM)
    anywhere = pl.BlockSpec(memory_space=pl.ANY)
    local_rows, gram = pl.pallas_call(
        gather_kernel,
        out_shape=(jax.ShapeDtypeStruct((SNAP, ROWS), f32), jax.ShapeDtypeStruct((SNAP, SNAP), f32)),
        in_specs=[anywhere],
        out_specs=(vmem, vmem),
        scratch_shapes=[
            pltpu.VMEM((2, 16, 128), f32), pltpu.VMEM((1, 16, 128), f32), pltpu.VMEM((2, 16, 128), f32),
            pltpu.VMEM((2, 16, 8, 128), f32), pltpu.VMEM((2, 8, 8, 128), f32),
            pltpu.VMEM((2, 8, 128), f32), pltpu.VMEM((2, 8, 128), f32),
            pltpu.SemaphoreType.DMA, pltpu.SemaphoreType.DMA((CHUNKS,)), pltpu.SemaphoreType.DMA((CHUNKS,)),
            pltpu.SemaphoreType.REGULAR((4,)), pltpu.SemaphoreType.REGULAR((3,)),
            pltpu.SemaphoreType.DMA((6,)), pltpu.SemaphoreType.DMA((6,)),
        ],
        compiler_params=pltpu.CompilerParams(collective_id=0, has_side_effects=True, vmem_limit_bytes=47 << 20),
        cost_estimate=pl.CostEstimate(flops=2 * 192 * 192 * ROWS, bytes_accessed=8 << 20, transcendentals=0),
    )(pressures)
    return pl.pallas_call(
        modes_kernel,
        out_shape=(jax.ShapeDtypeStruct((SNAP, SNAP), f32), jax.ShapeDtypeStruct((SNAP, ROWS), f32)),
        in_specs=[vmem, vmem],
        out_specs=(vmem, anywhere),
        scratch_shapes=[pltpu.VMEM((SNAP, ROWS), f32), pltpu.SemaphoreType.DMA],
        compiler_params=pltpu.CompilerParams(vmem_limit_bytes=40 << 20),
        cost_estimate=pl.CostEstimate(flops=2 * 384 * 64 * ROWS, bytes_accessed=8 << 20, transcendentals=0),
    )(local_rows, gram)


def solution(mesh):
    in_specs = (P("row", "grp"),)
    out_specs = (P(), P(None, ("grp", "row")))
    return jax.shard_map(shards, mesh=mesh, in_specs=in_specs, out_specs=out_specs, check_vma=False)
```

```python
import jax
import jax.numpy as jnp
from jax import lax
from jax.experimental import pallas as pl
from jax.experimental.pallas import tpu as pltpu
from jax.sharding import PartitionSpec as P

NSTEPS = 16
SNAP = 64
ROWS = 16384
FACES = 4194304
CHUNKS = 8
WIDTH = ROWS // CHUNKS
TILE = 1024
MESH = pl.DeviceIdType.MESH
f32, bf16 = jnp.float32, jnp.bfloat16


def split3(a):
    high = a.astype(bf16)
    rest = a - high.astype(f32)
    mid = rest.astype(bf16)
    low = (rest - mid.astype(f32)).astype(bf16)
    return high, mid, low


NEAR = [(0, 0, 1), (1, 0, 0), (0, 1, 0), (3, 0, 0), (0, 3, 0)]
NEXT = [(1, 1, 0), (3, 3, 0), (1, 3, 0), (3, 1, 0), (2, 0, 0), (0, 2, 0), (1, 0, 1), (0, 1, 1), (3, 0, 1), (0, 3, 1)]
FAR = [(2, 2, 1), (2, 2, 0), (2, 1, 0), (1, 2, 0), (2, 3, 0), (3, 2, 0), (2, 1, 1), (1, 2, 1), (2, 3, 1), (3, 2, 1),
       (1, 1, 1), (3, 3, 1), (1, 3, 1), (3, 1, 1), (2, 0, 1), (0, 2, 1)]


FAR_CHIPS = [(2, 2), (2, 1), (1, 2), (2, 3), (3, 2), (1, 1), (3, 3), (1, 3), (3, 1), (2, 0), (0, 2), (1, 0), (0, 1), (3, 0), (0, 3)]


def added(buf, count):
    terms = [buf[i] for i in range(count)]
    while len(terms) > 1:
        terms = [p + q for p, q in zip(terms[::2], terms[1::2])]
    return terms[0]


def gather_kernel(x_ref, land, g_ref, packed, pair, plane_buf, line_buf, plane_all, line_all, plane_sum, line_sum,
                  send_sem, recv_sem, own_sem, row_sem, grp_sem, red_send, red_recv):
    grp, me = lax.axis_index("grp"), lax.axis_index("row")
    mx, my, mc = me // 8, (me // 2) % 4, me % 2
    chip = me // 2
    at_x = [((mx + d) % 4) * 8 for d in range(4)]
    at_y = [((my + d) % 4) * 2 for d in range(4)]
    at_core = [mc, 1 - mc]
    above, below = (grp + 1) % 8, (grp + 7) % 8

    def row_place(offset):
        dx, dy, dc = offset
        straight = at_x[dx] + at_y[dy] + at_core[dc]
        if dx == dy:
            return straight
        return straight * (1 - mc) + (at_x[dy] + at_y[dx] + at_core[dc]) * mc

    def signal_near(sem):
        for offset in NEAR:
            pl.semaphore_signal(sem, inc=1, device_id=(grp, row_place(offset)), device_id_type=MESH)

    def signal_line(sem):
        pl.semaphore_signal(sem, inc=1, device_id=(above, me), device_id_type=MESH)
        pl.semaphore_signal(sem, inc=1, device_id=(below, me), device_id_type=MESH)

    barrier = pltpu.get_barrier_semaphore()
    signal_near(barrier)
    signal_line(barrier)
    pl.semaphore_wait(barrier, len(NEAR) + 2)
    signal_near(row_sem.at[0])
    signal_line(grp_sem.at[0])

    def rows_of(i, c):
        return land.at[pl.ds(pl.multiple_of(2 * i, 2), 2), pl.ds(pl.multiple_of(c * WIDTH, WIDTH), WIDTH)]

    def faces_of(j, c):
        return x_ref.at[:, pl.ds(pl.multiple_of(j * ROWS + c * WIDTH, WIDTH), WIDTH)]

    def wait_bytes(columns, sem):
        size = x_ref.at[:, pl.ds(0, columns)]
        pltpu.make_async_copy(size, size, sem).wait()

    def own(c):
        return pltpu.make_async_copy(faces_of(me, c), rows_of(me, c), own_sem.at[c])

    def send_chunks(first, last, offsets):
        def send(c, _):
            for offset in offsets:
                j = row_place(offset)
                pltpu.make_async_remote_copy(
                    src_ref=faces_of(j, c), dst_ref=rows_of(me, c), send_sem=send_sem, recv_sem=recv_sem.at[c],
                    device_id=(grp, j), device_id_type=MESH).start()
            return 0
        lax.fori_loop(first, last, send, 0)

    def next_round(r):
        pl.semaphore_wait(row_sem.at[r], len(NEAR))
        if r < 3:
            signal_near(row_sem.at[r + 1])

    send_chunks(0, CHUNKS, NEAR)
    next_round(0)
    send_chunks(0, 2, NEXT)
    next_round(1)
    send_chunks(2, 4, NEXT)
    next_round(2)
    send_chunks(4, CHUNKS, NEXT)
    next_round(3)
    send_chunks(0, CHUNKS, FAR)
    for c in range(CHUNKS):
        own(c).start()
    for r in range(3):
        pl.semaphore_wait(grp_sem.at[r], 2)
        if r < 2:
            signal_line(grp_sem.at[r + 1])

    total = jnp.zeros((3 * SNAP, 3 * SNAP), f32)
    for c in range(CHUNKS):
        own(c).wait()
        wait_bytes(31 * WIDTH, recv_sem.at[c])
        parts = jnp.concatenate(split3(land[:, c * WIDTH:(c + 1) * WIDTH]), axis=0)
        total = total + lax.dot_general(parts, parts, (((1,), (1,)), ((), ())), preferred_element_type=f32)
    a, b = SNAP, 2 * SNAP
    gram = total[:a, :a] + ((total[a:b, :a] + total[:a, a:b]) + (total[b:, :a] + total[:a, b:] + total[a:b, a:b]))

    def post(source, target, step, device):
        pltpu.make_async_remote_copy(
            src_ref=source, dst_ref=target, send_sem=red_send.at[step], recv_sem=red_recv.at[step],
            device_id=device, device_id_type=MESH).start()

    def first_round():
        line = [4, 3, 5, 2, 6, 1, 7]
        for i, (dx, dy) in enumerate(FAR_CHIPS):
            if i < len(line):
                post(line_sum.at[1], line_buf.at[grp], 2, ((grp + line[i]) % 8, me))
            post(plane_sum.at[0], plane_buf.at[chip], 1, (grp, at_x[dx] + at_y[dy] + mc))

    def to_plane(source, step):
        for dx, dy in FAR_CHIPS + [(0, 0)]:
            for dc in (0, 1):
                if dx or dy or dc:
                    post(source, plane_all.at[mc, chip], step, (grp, at_x[dx] + at_y[dy] + at_core[dc]))

    def to_line(source, step):
        for d in (4, 3, 5, 2, 6, 1, 7, 0):
            for dc in (0, 1):
                if d or dc:
                    post(source, line_all.at[mc, grp], step, ((grp + d) % 8, at_x[0] + at_y[0] + at_core[dc]))

    packed[...] = jnp.concatenate([gram[:32, :], gram[32:, :]], axis=1).reshape(2, 16, 128)
    post(packed.at[1 - mc], pair.at[0], 0, (grp, at_x[0] + at_y[0] + at_core[1]))
    wait_bytes(1024, red_recv.at[0])
    mine = packed[mc] + pair[0]
    plane_sum[0] = mine[:8]
    line_sum[1] = mine[8:]
    first_round()
    plane_buf[chip] = mine[:8]
    line_buf[grp] = mine[8:]
    wait_bytes(7 * 512, red_recv.at[2])
    quarter = added(line_buf, 8)
    plane_sum[1] = quarter
    to_plane(plane_sum.at[1], 4)
    plane_all[mc, chip] = quarter
    wait_bytes(15 * 512, red_recv.at[1])
    quarter = added(plane_buf, 16)
    line_sum[0] = quarter
    to_line(line_sum.at[0], 3)
    line_all[mc, grp] = quarter
    wait_bytes(31 * 512, red_recv.at[4])
    late = [added(plane_all.at[c], 16) for c in (0, 1)]
    wait_bytes(15 * 512, red_recv.at[3])
    early = [added(line_all.at[c], 8) for c in (0, 1)]
    summed = jnp.concatenate([early[0], late[0], early[1], late[1]], axis=0)
    g_ref[...] = jnp.concatenate([summed[:, :SNAP], summed[:, SNAP:]], axis=0)

    for step, columns in enumerate((1024, 15 * 512, 7 * 512, 15 * 512, 31 * 512)):
        wait_bytes(columns, red_send.at[step])
    wait_bytes(31 * ROWS, send_sem)


def modes_kernel(x_ref, g_ref, factor_ref, modes_hbm, out, sem):
    def times(p, q):
        return jnp.dot(p, q, precision=lax.Precision.HIGHEST, preferred_element_type=f32)

    gram = g_ref[...]
    down = lax.broadcasted_iota(jnp.int32, (SNAP, SNAP), 0)
    across = lax.broadcasted_iota(jnp.int32, (SNAP, SNAP), 1)
    eye = jnp.where(down == across, 1.0, 0.0).astype(f32)
    lane = lax.broadcasted_iota(jnp.int32, (1, SNAP), 1)
    square = jnp.sum(jnp.sum(gram * eye, axis=0, keepdims=True), axis=1, keepdims=True) + 1e-6
    shape, inverse = gram / square, eye
    rest, rows = gram, []
    for step in range(NSTEPS):
        factor = 1.5 * eye - 0.5 * shape
        if step < NSTEPS - 1:
            shape_square = times(shape, shape)
        inverse = factor if step == 0 else times(inverse, factor)
        if step < NSTEPS - 1:
            shape = times(1.5 * shape - 0.5 * shape_square, factor)
        for k in range(step * SNAP // NSTEPS, (step + 1) * SNAP // NSTEPS):
            scale = lax.rsqrt(rest[k:k + 1, k:k + 1])
            row = rest[k:k + 1, :] * scale
            rows.append(jnp.where(lane >= k, row, 0.0))
            rest = rest - (rest[:, k:k + 1] * scale) * row
    root = float(FACES) ** 0.5
    factor_ref[...] = jnp.concatenate(rows, axis=0) * (1.0 / root)
    mixer = inverse * (root * lax.rsqrt(square))
    high, mid, low = split3(mixer)
    none = jnp.zeros_like(high)
    left = jnp.concatenate([jnp.concatenate([high, high, high, mid], axis=1),
                            jnp.concatenate([low, mid, none, none], axis=1)], axis=0)

    def tile(i, _):
        cols = pl.ds(pl.multiple_of(i * TILE, TILE), TILE)
        h, m, l = split3(x_ref[:, cols])
        both = jnp.dot(left, jnp.concatenate([h, m, l, h], axis=0), preferred_element_type=f32)
        out[:, cols] = both[:SNAP] + both[SNAP:]
        pltpu.make_async_copy(out.at[:, cols], modes_hbm.at[:, cols], sem).start()
        return 0
    lax.fori_loop(0, ROWS // TILE, tile, 0, unroll=ROWS // TILE)
    pltpu.make_async_copy(out, modes_hbm, sem).wait()


def shards(pressures):
    vmem = pl.BlockSpec(memory_space=pltpu.VMEM)
    anywhere = pl.BlockSpec(memory_space=pl.ANY)
    local_rows, gram = pl.pallas_call(
        gather_kernel,
        out_shape=(jax.ShapeDtypeStruct((SNAP, ROWS), f32), jax.ShapeDtypeStruct((SNAP, SNAP), f32)),
        in_specs=[anywhere],
        out_specs=(vmem, vmem),
        scratch_shapes=[
            pltpu.VMEM((2, 16, 128), f32), pltpu.VMEM((1, 16, 128), f32),
            pltpu.VMEM((16, 8, 128), f32), pltpu.VMEM((8, 8, 128), f32),
            pltpu.VMEM((2, 16, 8, 128), f32), pltpu.VMEM((2, 8, 8, 128), f32),
            pltpu.VMEM((2, 8, 128), f32), pltpu.VMEM((2, 8, 128), f32),
            pltpu.SemaphoreType.DMA, pltpu.SemaphoreType.DMA((CHUNKS,)), pltpu.SemaphoreType.DMA((CHUNKS,)),
            pltpu.SemaphoreType.REGULAR((4,)), pltpu.SemaphoreType.REGULAR((3,)),
            pltpu.SemaphoreType.DMA((5,)), pltpu.SemaphoreType.DMA((5,)),
        ],
        compiler_params=pltpu.CompilerParams(collective_id=0, has_side_effects=True, vmem_limit_bytes=47 << 20),
        cost_estimate=pl.CostEstimate(flops=2 * 192 * 192 * ROWS, bytes_accessed=8 << 20, transcendentals=0),
    )(pressures)
    return pl.pallas_call(
        modes_kernel,
        out_shape=(jax.ShapeDtypeStruct((SNAP, SNAP), f32), jax.ShapeDtypeStruct((SNAP, ROWS), f32)),
        in_specs=[vmem, vmem],
        out_specs=(vmem, anywhere),
        scratch_shapes=[pltpu.VMEM((SNAP, ROWS), f32), pltpu.SemaphoreType.DMA],
        compiler_params=pltpu.CompilerParams(vmem_limit_bytes=40 << 20),
        cost_estimate=pl.CostEstimate(flops=2 * 384 * 64 * ROWS, bytes_accessed=8 << 20, transcendentals=0),
    )(local_rows, gram)


def solution(mesh):
    in_specs = (P("row", "grp"),)
    out_specs = (P(), P(None, ("grp", "row")))
    return jax.shard_map(shards, mesh=mesh, in_specs=in_specs, out_specs=out_specs, check_vma=False)
```

```python
import jax
import jax.numpy as jnp
from jax import lax
from jax.experimental import pallas as pl
from jax.experimental.pallas import tpu as pltpu
from jax.sharding import PartitionSpec as P

NSTEPS = 16
SNAP = 64
ROWS = 16384
FACES = 4194304
CHUNKS = 8
WIDTH = ROWS // CHUNKS
TILE = 1024
MESH = pl.DeviceIdType.MESH
f32, bf16 = jnp.float32, jnp.bfloat16


def split3(a):
    high = a.astype(bf16)
    rest = a - high.astype(f32)
    mid = rest.astype(bf16)
    low = (rest - mid.astype(f32)).astype(bf16)
    return high, mid, low


NEAR = [(0, 0, 1), (1, 0, 0), (0, 1, 0), (3, 0, 0), (0, 3, 0)]
NEXT = [(1, 1, 0), (3, 3, 0), (1, 3, 0), (3, 1, 0), (2, 0, 0), (0, 2, 0), (1, 0, 1), (0, 1, 1), (3, 0, 1), (0, 3, 1)]
FAR = [(2, 2, 1), (2, 2, 0), (2, 1, 0), (1, 2, 0), (2, 3, 0), (3, 2, 0), (2, 1, 1), (1, 2, 1), (2, 3, 1), (3, 2, 1),
       (1, 1, 1), (3, 3, 1), (1, 3, 1), (3, 1, 1), (2, 0, 1), (0, 2, 1)]


FAR_CHIPS = [(2, 2), (2, 1), (1, 2), (2, 3), (3, 2), (1, 1), (3, 3), (1, 3), (3, 1), (2, 0), (0, 2), (1, 0), (0, 1), (3, 0), (0, 3)]


def added(buf, count):
    terms = [buf[i] for i in range(count)]
    while len(terms) > 1:
        terms = [p + q for p, q in zip(terms[::2], terms[1::2])]
    return terms[0]


def gather_kernel(x_ref, land, g_ref, packed, plane_buf, line_buf, plane_all, line_all, plane_sum, line_sum,
                  send_sem, recv_sem, own_sem, row_sem, grp_sem, red_send, red_recv):
    grp, me = lax.axis_index("grp"), lax.axis_index("row")
    mx, my, mc = me // 8, (me // 2) % 4, me % 2
    chip = me // 2
    at_x = [((mx + d) % 4) * 8 for d in range(4)]
    at_y = [((my + d) % 4) * 2 for d in range(4)]
    at_core = [mc, 1 - mc]
    above, below = (grp + 1) % 8, (grp + 7) % 8

    def row_place(offset):
        dx, dy, dc = offset
        straight = at_x[dx] + at_y[dy] + at_core[dc]
        if dx == dy:
            return straight
        return straight * (1 - mc) + (at_x[dy] + at_y[dx] + at_core[dc]) * mc

    def signal_near(sem):
        for offset in NEAR:
            pl.semaphore_signal(sem, inc=1, device_id=(grp, row_place(offset)), device_id_type=MESH)

    def signal_line(sem):
        pl.semaphore_signal(sem, inc=1, device_id=(above, me), device_id_type=MESH)
        pl.semaphore_signal(sem, inc=1, device_id=(below, me), device_id_type=MESH)

    barrier = pltpu.get_barrier_semaphore()
    signal_near(barrier)
    signal_line(barrier)
    pl.semaphore_wait(barrier, len(NEAR) + 2)
    signal_near(row_sem.at[0])
    signal_line(grp_sem.at[0])

    def rows_of(i, c):
        return land.at[pl.ds(pl.multiple_of(2 * i, 2), 2), pl.ds(pl.multiple_of(c * WIDTH, WIDTH), WIDTH)]

    def faces_of(j, c):
        return x_ref.at[:, pl.ds(pl.multiple_of(j * ROWS + c * WIDTH, WIDTH), WIDTH)]

    def wait_bytes(columns, sem):
        size = x_ref.at[:, pl.ds(0, columns)]
        pltpu.make_async_copy(size, size, sem).wait()

    def own(c):
        return pltpu.make_async_copy(faces_of(me, c), rows_of(me, c), own_sem.at[c])

    def send_chunks(first, last, offsets):
        def send(c, _):
            for offset in offsets:
                j = row_place(offset)
                pltpu.make_async_remote_copy(
                    src_ref=faces_of(j, c), dst_ref=rows_of(me, c), send_sem=send_sem, recv_sem=recv_sem.at[c],
                    device_id=(grp, j), device_id_type=MESH).start()
            return 0
        lax.fori_loop(first, last, send, 0)

    def next_round(r):
        pl.semaphore_wait(row_sem.at[r], len(NEAR))
        if r < 3:
            signal_near(row_sem.at[r + 1])

    send_chunks(0, CHUNKS, NEAR)
    next_round(0)
    send_chunks(0, 2, NEXT)
    next_round(1)
    send_chunks(2, 4, NEXT)
    next_round(2)
    send_chunks(4, CHUNKS, NEXT)
    next_round(3)
    send_chunks(0, CHUNKS, FAR)
    for c in range(CHUNKS):
        own(c).start()
    for r in range(4):
        pl.semaphore_wait(grp_sem.at[r], 2)
        if r < 3:
            signal_line(grp_sem.at[r + 1])

    total = jnp.zeros((3 * SNAP, 3 * SNAP), f32)
    for c in range(CHUNKS):
        own(c).wait()
        wait_bytes(31 * WIDTH, recv_sem.at[c])
        parts = jnp.concatenate(split3(land[:, c * WIDTH:(c + 1) * WIDTH]), axis=0)
        total = total + lax.dot_general(parts, parts, (((1,), (1,)), ((), ())), preferred_element_type=f32)
    a, b = SNAP, 2 * SNAP
    gram = total[:a, :a] + ((total[a:b, :a] + total[:a, a:b]) + (total[b:, :a] + total[:a, b:] + total[a:b, a:b]))

    def post(source, target, step, device):
        pltpu.make_async_remote_copy(
            src_ref=source, dst_ref=target, send_sem=red_send.at[step], recv_sem=red_recv.at[step],
            device_id=device, device_id_type=MESH).start()

    def first_round():
        line = [4, 3, 5, 2, 6, 1, 7, 0]
        for i, (dx, dy) in enumerate(FAR_CHIPS + [(0, 0)]):
            for dc in (0, 1):
                owner = at_core[dc]
                if i < len(line) and (line[i] or dc):
                    post(packed.at[owner, 1], line_buf.at[mc, grp], 1,
                         ((grp + line[i]) % 8, at_x[0] + at_y[0] + owner))
                if dx or dy or dc:
                    post(packed.at[owner, 0], plane_buf.at[mc, chip], 0, (grp, at_x[dx] + at_y[dy] + owner))

    def to_plane(source, step):
        for dx, dy in FAR_CHIPS + [(0, 0)]:
            for dc in (0, 1):
                if dx or dy or dc:
                    post(source, plane_all.at[mc, chip], step, (grp, at_x[dx] + at_y[dy] + at_core[dc]))

    def to_line(source, step):
        for d in (4, 3, 5, 2, 6, 1, 7, 0):
            for dc in (0, 1):
                if d or dc:
                    post(source, line_all.at[mc, grp], step, ((grp + d) % 8, at_x[0] + at_y[0] + at_core[dc]))

    packed[...] = jnp.concatenate([gram[:32, :], gram[32:, :]], axis=1).reshape(2, 2, 8, 128)
    first_round()
    plane_buf[mc, chip] = packed[mc, 0]
    line_buf[mc, grp] = packed[mc, 1]
    wait_bytes(15 * 512, red_recv.at[1])
    quarter = added(line_buf.at[0], 8) + added(line_buf.at[1], 8)
    plane_sum[...] = quarter
    to_plane(plane_sum, 3)
    plane_all[mc, chip] = quarter
    wait_bytes(31 * 512, red_recv.at[0])
    quarter = added(plane_buf.at[0], 16) + added(plane_buf.at[1], 16)
    line_sum[...] = quarter
    to_line(line_sum, 2)
    line_all[mc, grp] = quarter
    wait_bytes(31 * 512, red_recv.at[3])
    late = [added(plane_all.at[c], 16) for c in (0, 1)]
    wait_bytes(15 * 512, red_recv.at[2])
    early = [added(line_all.at[c], 8) for c in (0, 1)]
    summed = jnp.concatenate([early[0], late[0], early[1], late[1]], axis=0)
    g_ref[...] = jnp.concatenate([summed[:, :SNAP], summed[:, SNAP:]], axis=0)

    for step, columns in enumerate((31 * 512, 15 * 512, 15 * 512, 31 * 512)):
        wait_bytes(columns, red_send.at[step])
    wait_bytes(31 * ROWS, send_sem)


def modes_kernel(x_ref, g_ref, factor_ref, modes_hbm, out, sem):
    def times(p, q):
        return jnp.dot(p, q, precision=lax.Precision.HIGHEST, preferred_element_type=f32)

    gram = g_ref[...]
    down = lax.broadcasted_iota(jnp.int32, (SNAP, SNAP), 0)
    across = lax.broadcasted_iota(jnp.int32, (SNAP, SNAP), 1)
    eye = jnp.where(down == across, 1.0, 0.0).astype(f32)
    lane = lax.broadcasted_iota(jnp.int32, (1, SNAP), 1)
    square = jnp.sum(jnp.sum(gram * eye, axis=0, keepdims=True), axis=1, keepdims=True) + 1e-6
    shape, inverse = gram / square, eye
    rest, rows = gram, []
    for step in range(NSTEPS):
        factor = 1.5 * eye - 0.5 * shape
        if step < NSTEPS - 1:
            shape_square = times(shape, shape)
        inverse = factor if step == 0 else times(inverse, factor)
        if step < NSTEPS - 1:
            shape = times(1.5 * shape - 0.5 * shape_square, factor)
        for k in range(step * SNAP // NSTEPS, (step + 1) * SNAP // NSTEPS):
            scale = lax.rsqrt(rest[k:k + 1, k:k + 1])
            row = rest[k:k + 1, :] * scale
            rows.append(jnp.where(lane >= k, row, 0.0))
            rest = rest - (rest[:, k:k + 1] * scale) * row
    root = float(FACES) ** 0.5
    factor_ref[...] = jnp.concatenate(rows, axis=0) * (1.0 / root)
    mixer = inverse * (root * lax.rsqrt(square))
    high, mid, low = split3(mixer)
    none = jnp.zeros_like(high)
    left = jnp.concatenate([jnp.concatenate([high, high, high, mid], axis=1),
                            jnp.concatenate([low, mid, none, none], axis=1)], axis=0)

    def tile(i, _):
        cols = pl.ds(pl.multiple_of(i * TILE, TILE), TILE)
        h, m, l = split3(x_ref[:, cols])
        both = jnp.dot(left, jnp.concatenate([h, m, l, h], axis=0), preferred_element_type=f32)
        out[:, cols] = both[:SNAP] + both[SNAP:]
        pltpu.make_async_copy(out.at[:, cols], modes_hbm.at[:, cols], sem).start()
        return 0
    lax.fori_loop(0, ROWS // TILE, tile, 0, unroll=ROWS // TILE)
    pltpu.make_async_copy(out, modes_hbm, sem).wait()


def shards(pressures):
    vmem = pl.BlockSpec(memory_space=pltpu.VMEM)
    anywhere = pl.BlockSpec(memory_space=pl.ANY)
    local_rows, gram = pl.pallas_call(
        gather_kernel,
        out_shape=(jax.ShapeDtypeStruct((SNAP, ROWS), f32), jax.ShapeDtypeStruct((SNAP, SNAP), f32)),
        in_specs=[anywhere],
        out_specs=(vmem, vmem),
        scratch_shapes=[
            pltpu.VMEM((2, 2, 8, 128), f32),
            pltpu.VMEM((2, 16, 8, 128), f32), pltpu.VMEM((2, 8, 8, 128), f32),
            pltpu.VMEM((2, 16, 8, 128), f32), pltpu.VMEM((2, 8, 8, 128), f32),
            pltpu.VMEM((8, 128), f32), pltpu.VMEM((8, 128), f32),
            pltpu.SemaphoreType.DMA, pltpu.SemaphoreType.DMA((CHUNKS,)), pltpu.SemaphoreType.DMA((CHUNKS,)),
            pltpu.SemaphoreType.REGULAR((4,)), pltpu.SemaphoreType.REGULAR((4,)),
            pltpu.SemaphoreType.DMA((4,)), pltpu.SemaphoreType.DMA((4,)),
        ],
        compiler_params=pltpu.CompilerParams(collective_id=0, has_side_effects=True, vmem_limit_bytes=47 << 20),
        cost_estimate=pl.CostEstimate(flops=2 * 192 * 192 * ROWS, bytes_accessed=8 << 20, transcendentals=0),
    )(pressures)
    return pl.pallas_call(
        modes_kernel,
        out_shape=(jax.ShapeDtypeStruct((SNAP, SNAP), f32), jax.ShapeDtypeStruct((SNAP, ROWS), f32)),
        in_specs=[vmem, vmem],
        out_specs=(vmem, anywhere),
        scratch_shapes=[pltpu.VMEM((SNAP, ROWS), f32), pltpu.SemaphoreType.DMA],
        compiler_params=pltpu.CompilerParams(vmem_limit_bytes=40 << 20),
        cost_estimate=pl.CostEstimate(flops=2 * 384 * 64 * ROWS, bytes_accessed=8 << 20, transcendentals=0),
    )(local_rows, gram)


def solution(mesh):
    in_specs = (P("row", "grp"),)
    out_specs = (P(), P(None, ("grp", "row")))
    return jax.shard_map(shards, mesh=mesh, in_specs=in_specs, out_specs=out_specs, check_vma=False)
```
